256 devices in a mesh: row: 8 (over z_hi, y), col: 32 (over x, z_lo, core).
Axes of the slice: x: 4, y: 4, z: 8 (z_hi: 2, z_lo: 4; z = z_hi * 4 + z_lo), core: 2. Of those that a mesh axis runs over, the one named last changes fastest.
Arguments:
- active_matrix: float32 [16384, 16384], P('row', 'col'), may hold values from -6 to 6
- schur_rows: float32 [2048, 16384], P('row', 'col'), may hold values from -6 to 6
- accum_first: float32 [32, 512, 512], P('row', 'col'), may hold values from -1 to 1, as said below
- accum_second: float32 [32, 512, 512], P('row', 'col'), may hold values from -1 to 1, as said below
Outputs:
- matrix_out: float32 [16384, 16384], P('row', 'col')
- schur_out: float32 [2048, 16384], P('row', 'col')
The draws below stay inside these ranges and needn't reach their ends.
Inputs may be any that keep to these rules, and one draw needn't show every extreme that they name: `accum_first`: each of the 32 blocks of order 512 is an orthogonal matrix. `accum_second`: each of the 32 blocks of order 512 is an orthogonal matrix.
All inputs are finite; a program needn't handle non-finite values.
Results may differ from the reference program's by a relative error of at most 0.000098.
Values sent between devices are 32-bit elements; how exact they have to be, the bound alone decides.
A program may use at most 128 MiB of HBM per device.

```python
import jax
import jax.numpy as jnp
from jax import lax

N = 16384
W = 512
K = 32
ZROWS = 2048


def orthogonal_blocks(key):
    normal = jax.random.normal(key, (K, W, W), jnp.float32)
    basis, upper = jnp.linalg.qr(normal)
    signs = jnp.sign(jnp.diagonal(upper, axis1=1, axis2=2))
    signs = jnp.where(signs == 0, 1.0, signs)
    return basis * signs[:, None, :]


def draw_accum_first(key, part):
    return orthogonal_blocks(jax.random.fold_in(key, 11))


def draw_accum_second(key, part):
    return orthogonal_blocks(jax.random.fold_in(key, 23))


def block_levels(own_key, extent, cuts, least, largest):
    factor_of = 1.0
    for position, shards_of in cuts:
        steps = jax.random.uniform(jax.random.fold_in(jax.random.fold_in(own_key, 6), position), (shards_of,), jnp.float32, least / len(cuts), largest / len(cuts))
        factor_of = factor_of * jnp.repeat(jnp.exp(steps), extent[position] // shards_of).reshape((-1,) + (1,) * (len(extent) - 1 - position))
    return factor_of


def bell_draw(key, shape, scale, reach, shards=(), kind=jnp.bfloat16):
    gain = block_levels(key, shape, shards, -0.22, 0.18) if shards else 1.0
    entries = jax.random.normal(key, shape, jnp.float32) * scale * gain
    return jnp.minimum(jnp.maximum(entries, -reach), reach).astype(kind)


def setup_inputs(seed: int = 0) -> dict:
    seeds = jax.random.split(jax.random.key(seed), 5)
    return {
        "active_matrix": bell_draw(seeds[0], (N, N), 1.0, 6.0, ((0, 8), (1, 32)), jnp.float32),
        "schur_rows": bell_draw(seeds[1], (ZROWS, N), 1.0, 6.0, ((0, 8), (1, 32)), jnp.float32),
        "accum_first": draw_accum_first(jax.random.fold_in(seeds[4], 71), 0),
        "accum_second": draw_accum_second(jax.random.fold_in(seeds[4], 71), 0),
    }


def left_apply(blocks, matrix):
    shaped = matrix.reshape(K, W, matrix.shape[1])
    out = jnp.einsum('kij,kin->kjn', blocks, shaped, precision=lax.Precision.HIGHEST)
    return out.reshape(N, matrix.shape[1])

def right_apply(matrix, blocks):
    rows = matrix.shape[0]
    shaped = matrix.reshape(rows, K, W)
    out = jnp.einsum('nki,kij->nkj', shaped, blocks, precision=lax.Precision.HIGHEST)
    return out.reshape(rows, N)

def reference(active_matrix, schur_rows, accum_first, accum_second):
    first_h = right_apply(left_apply(accum_first, active_matrix), accum_first)
    first_z = right_apply(schur_rows, accum_first)
    offset = W // 2
    rolled = jnp.roll(first_h, offset, (0, 1))
    second_h = right_apply(left_apply(accum_second, rolled), accum_second)
    matrix_out = jnp.roll(second_h, -offset, (0, 1))
    rolled_z = jnp.roll(first_z, offset, 1)
    schur_out = jnp.roll(right_apply(rolled_z, accum_second), -offset, 1)
    return (matrix_out, schur_out)
```

```python
import jax
import jax.numpy as jnp
from jax import lax
from jax.experimental import pallas as pl
from jax.experimental.pallas import tpu as pltpu
from jax.sharding import PartitionSpec as P

MESH = pl.DeviceIdType.MESH
F32 = jnp.float32
BF16 = jnp.bfloat16

W = 512
HALF = 256
ROWS = 2048
ZR = 256
BLOCKS = (ROWS + ZR) // 256


def split(a):
    high = a.astype(BF16)
    low = (a - high.astype(F32)).astype(BF16)
    return high, low


def product(a, b, dims):
    (a_high, a_low), (b_high, b_low) = a, b

    def dot(left, right):
        return lax.dot_general(left, right, (dims, ((), ())), preferred_element_type=F32)

    return (dot(a_low, b_high) + dot(a_high, b_low)) + dot(a_high, b_high)


def plain(a, b):
    return product(a, b, ((1,), (0,)))


def turned(a, b):
    return product(a, b, ((0,), (0,)))


def remote(src, dst, send, recv, device):
    return pltpu.make_async_remote_copy(
        src_ref=src, dst_ref=dst, send_sem=send, recv_sem=recv, device_id=device, device_id_type=MESH
    )


def at(start, size):
    return pl.ds(pl.multiple_of(start, size), size)


def block_of(position):
    return jnp.where(
        position < 2, position, jnp.where(position < 4, position + 4, jnp.where(position < 8, position - 2, 8))
    )


def window_of(position):
    return jnp.where(position == 0, 0, jnp.where(position == 1, 3, position - 1))


def kernel(
    h_ref, z_ref, u_ref, v_ref, ho_ref, zo_ref,
    tile, piece, gathered, column, col_high, col_low, wide, t_high, t_low, tall, result,
    load_sem, a_send, a_recv, shift_sem, sib_send, sib_recv, own_sem, y_send, y_recv,
    z_send, z_recv, x_send, x_recv, f_send, f_recv, c_send, c_recv, d_send, d_recv, out_sem,
):
    r, c = lax.axis_index("row"), lax.axis_index("col")
    hi, y = r // 4, r % 4
    x, z, core = c // 8, (c // 2) % 4, c % 2
    sibling = (r, c + 1 - 2 * core)
    y_next, y_prev = (hi * 4 + (y + 1) % 4, c), (hi * 4 + (y + 3) % 4, c)
    x_next, x_prev = (r, (c + 8) % 32), (r, (c + 24) % 32)
    z_other = [(r, 8 * x + 2 * ((z + d) % 4) + core) for d in (1, 2, 3)]
    c_next, c_prev = (r, (c + 1) % 32), (r, (c + 31) % 32)
    r_next, r_prev = ((r + 1) % 8, c), ((r + 7) % 8, c)
    source_row = c // 4
    to_self = jnp.logical_and(source_row == r, x == y)
    half = at(core * 1024, 1024)
    other_half = at(1024 - core * 1024, 1024)

    loads = [
        pltpu.make_async_copy(h_ref, tile.at[pl.ds(0, ROWS)], load_sem.at[0]),
        pltpu.make_async_copy(z_ref, tile.at[pl.ds(ROWS, ZR)], load_sem.at[1]),
    ]
    u_loads = [
        pltpu.make_async_copy(u_ref.at[k], piece.at[0, :, pl.ds(W * k, W)], load_sem.at[2 + k]) for k in range(4)
    ]
    v_loads = [
        pltpu.make_async_copy(
            v_ref.at[0, :, pl.ds(HALF, HALF)], piece.at[1, :, pl.ds(0, HALF)], load_sem.at[6]
        )
    ] + [
        pltpu.make_async_copy(v_ref.at[k], piece.at[1, :, pl.ds(W * k - HALF, W)], load_sem.at[6 + k])
        for k in range(1, 4)
    ]
    for copy in u_loads + v_loads + loads:
        copy.start()

    barrier = pltpu.get_barrier_semaphore()
    for device in [sibling, y_next, y_prev, x_next, x_prev, c_next, c_prev, r_next, r_prev] + z_other:
        pl.semaphore_signal(barrier, inc=1, device_id=device, device_id_type=MESH)
    for i in range(8):
        source = 8 * y + i

        @pl.when(jnp.logical_not(jnp.logical_and(source_row == r, source == c)))
        def _():
            pl.semaphore_signal(barrier, inc=1, device_id=(source_row, source), device_id_type=MESH)

    pl.semaphore_wait(barrier, 20 - to_self.astype(jnp.int32))

    waits = []

    shift = remote(
        v_ref.at[0, :, pl.ds(0, HALF)], piece.at[1, :, pl.ds(ROWS - HALF, HALF)],
        shift_sem.at[0], shift_sem.at[1], r_prev,
    )
    shift.start()

    def spread_start(t):
        for k in range(4):
            for other in range(2):
                src = piece.at[t, :, pl.ds(W * k, W)]
                dst = column.at[t, at(16 * c, 16), :]
                here = jnp.logical_and(jnp.logical_and(other == hi, x == y), 4 * r + k == c)

                @pl.when(here)
                def _():
                    pltpu.make_async_copy(src, dst, a_recv.at[t]).start()

                @pl.when(jnp.logical_not(here))
                def _():
                    remote(
                        src, dst, a_send.at[t, 2 * k + other], a_recv.at[t], (4 * other + x, 4 * r + k)
                    ).start()

    def spread_sent(t):
        for k in range(4):
            for other in range(2):
                src = piece.at[t, :, pl.ds(W * k, W)]
                dst = column.at[t, at(16 * c, 16), :]
                here = jnp.logical_and(jnp.logical_and(other == hi, x == y), 4 * r + k == c)

                @pl.when(jnp.logical_not(here))
                def _():
                    remote(
                        src, dst, a_send.at[t, 2 * k + other], a_recv.at[t], (4 * other + x, 4 * r + k)
                    ).wait_send()

    def spread_arrived(t):
        group = column.at[t, at(128 * y, 128), :]
        pltpu.make_async_copy(group, group, a_recv.at[t]).wait()

    def ring(t, me, next_device, prev_device, region, part, send, recv):
        def copies(i):
            back, front, far = (i + 3) % 4, (i + 1) % 4, (i + 2) % 4
            out = [
                remote(region(i), region(i), send.at[t, 0], recv.at[t, 0], next_device),
                remote(region(i), region(i), send.at[t, 1], recv.at[t, 1], prev_device),
                remote(part(back, 0), part(back, 0), send.at[t, 2], recv.at[t, 2], next_device),
                remote(part(front, 1), part(front, 1), send.at[t, 3], recv.at[t, 3], prev_device),
            ]
            arrivals = [
                remote(region(back), region(back), send.at[t, 0], recv.at[t, 0], next_device),
                remote(region(front), region(front), send.at[t, 1], recv.at[t, 1], prev_device),
                remote(part(far, 0), part(far, 0), send.at[t, 2], recv.at[t, 2], next_device),
                remote(part(far, 1), part(far, 1), send.at[t, 3], recv.at[t, 3], prev_device),
            ]
            return out, arrivals

        return copies(me)

    y_rings = [
        ring(
            t, y, y_next, y_prev,
            lambda j, t=t: column.at[t, at(128 * j, 128), :],
            lambda j, s, t=t: column.at[t, at(128 * j + 64 * s, 64), :],
            y_send, y_recv,
        )
        for t in range(2)
    ]
    x_rings = [
        ring(
            t, x, x_next, x_prev,
            lambda j, t=t: gathered.at[t, at(128 * j, 128), half],
            lambda j, s, t=t: gathered.at[t, at(128 * j + 64 * s, 64), half],
            x_send, x_recv,
        )
        for t in range(2)
    ]

    def start(copy):
        copy.start()
        waits.append(copy)

    def sibling_start(t):
        start(
            remote(
                piece.at[t, :, other_half], gathered.at[t, at(16 * c, 16), other_half],
                sib_send.at[t], sib_recv.at[t], sibling,
            )
        )
        pltpu.make_async_copy(piece.at[t, :, half], gathered.at[t, at(16 * c, 16), half], own_sem.at[t]).start()

    def sibling_arrived(t):
        rows = at(16 * (c + 1 - 2 * core), 16)
        remote(
            piece.at[t, :, half], gathered.at[t, rows, half], sib_send.at[t], sib_recv.at[t], sibling
        ).wait_recv()
        pltpu.make_async_copy(piece.at[t, :, half], gathered.at[t, at(16 * c, 16), half], own_sem.at[t]).wait()

    def z_start(t):
        ours = gathered.at[t, at(32 * (c // 2), 32), half]
        for i in range(3):
            start(remote(ours, ours, z_send.at[t, i], z_recv.at[t, i], z_other[i]))

    def z_arrived(t):
        for i in range(3):
            theirs = gathered.at[t, at(32 * (4 * x + (z + 3 - i) % 4), 32), half]
            remote(theirs, theirs, z_send.at[t, i], z_recv.at[t, i], z_other[i]).wait_recv()

    def forward(t, j):
        group = gathered.at[t, at(128 * ((x + j) % 4), 128), half]
        start(remote(group, group, f_send.at[t, j], f_recv.at[t, j], sibling))

    def forwarded(t):
        for j in range(4):
            group = gathered.at[t, at(128 * ((x + j) % 4), 128), other_half]
            remote(group, group, f_send.at[t, j], f_recv.at[t, j], sibling).wait_recv()

    def ring_first(ring):
        out, _ = ring
        start(out[0])
        start(out[1])

    def ring_second(ring):
        out, arrivals = ring
        arrivals[0].wait_recv()
        start(out[2])
        arrivals[1].wait_recv()
        start(out[3])

    def ring_last(ring):
        _, arrivals = ring
        arrivals[2].wait_recv()
        arrivals[3].wait_recv()

    def split_column(t):
        high, low = split(column[t])
        col_high[t] = high
        col_low[t] = low

    def strip_copies(b):
        rows = at(256 * b, 256)
        return (
            remote(
                wide.at[rows, pl.ds(256, 256)], wide.at[rows, pl.ds(768, 256)],
                c_send.at[0, b], c_recv.at[0, b], c_prev,
            ),
            remote(
                wide.at[rows, pl.ds(512, 256)], wide.at[rows, pl.ds(0, 256)],
                c_send.at[1, b], c_recv.at[1, b], c_next,
            ),
        )

    def right_first(low, high):
        @pl.loop(low, high)
        def _(position):
            b = block_of(position)
            rows = at(256 * b, 256)
            wide[rows, pl.ds(256, 512)] = plain(split(tile[rows, :]), (col_high[0], col_low[0]))
            for copy in strip_copies(b):
                copy.start()

    def right_second(b, store):
        rows = at(256 * b, 256)
        for copy in strip_copies(b):
            copy.wait_recv()
        for s in range(2):
            cols = pl.ds(256 * s, 256)
            store(
                cols,
                plain(split(wide[rows, pl.ds(512 * s, 512)]), (col_high[1, :, cols], col_low[1, :, cols])),
            )

    row_copies = (
        remote(
            tall.at[pl.ds(256, 256)], tall.at[pl.ds(2304, 256)], d_send.at[0], d_recv.at[0], r_prev
        ),
        remote(
            tall.at[pl.ds(2048, 256)], tall.at[pl.ds(0, 256)], d_send.at[1], d_recv.at[1], r_next
        ),
    )

    def window(position):
        k = window_of(position)

        @pl.loop(0, 2)
        def _(s):
            def store(cols, value):
                high, low = split(value)
                t_high[at(256 * s, 256), cols] = high
                t_low[at(256 * s, 256), cols] = low

            right_second(2 * k + s, store)

        @pl.loop(0, 2)
        def _(s):
            start_row = 512 * k + 256 * s
            tall[at(256 + start_row, 256), :] = turned(
                split(gathered[0, :, at(start_row, 256)]), (t_high[...], t_low[...])
            )

        if position == 0:
            start(row_copies[0])
        if position == 1:
            start(row_copies[1])

    def out_copy(j):
        return pltpu.make_async_copy(
            result.at[at(256 * j, 256)], ho_ref.at[at(256 * j, 256)], out_sem.at[j]
        )

    def left_second(low, high):
        @pl.loop(low, high)
        def _(j):
            result[at(256 * j, 256), :] = turned(
                split(gathered[1, :, at(256 * j, 256)]), split(tall[at(512 * ((j + 1) // 2), 512), :])
            )
            out_copy(j).start()

    for copy in u_loads:
        copy.wait()
    spread_start(0)
    sibling_start(0)
    spread_arrived(0)
    ring_first(y_rings[0])
    sibling_arrived(0)
    z_start(0)
    for copy in v_loads:
        copy.wait()
    shift.wait_recv()
    spread_start(1)
    sibling_start(1)
    ring_second(y_rings[0])
    sibling_arrived(1)
    z_start(1)
    z_arrived(0)
    ring_first(x_rings[0])
    forward(0, 0)
    for copy in loads:
        copy.wait()
    ring_last(y_rings[0])
    split_column(0)
    right_first(0, 4)
    spread_arrived(1)
    ring_first(y_rings[1])
    ring_second(x_rings[0])
    forward(0, 3)
    forward(0, 1)
    right_first(4, 9)
    ring_second(y_rings[1])
    z_arrived(1)
    ring_first(x_rings[1])
    forward(1, 0)
    ring_last(x_rings[0])
    forward(0, 2)
    ring_last(y_rings[1])
    split_column(1)
    forwarded(0)
    window(0)
    ring_second(x_rings[1])
    forward(1, 3)
    forward(1, 1)
    window(1)
    ring_last(x_rings[1])
    forward(1, 2)
    window(2)
    forwarded(1)
    left_second(1, 3)
    window(3)
    left_second(3, 7)

    def store_z(cols, value):
        result[pl.ds(ROWS, ZR), cols] = value

    right_second(8, store_z)
    z_out = pltpu.make_async_copy(result.at[pl.ds(ROWS, ZR)], zo_ref, out_sem.at[8])
    z_out.start()
    row_copies[1].wait_recv()
    left_second(0, 1)
    row_copies[0].wait_recv()
    left_second(7, 8)

    for copy in waits:
        copy.wait_send()
    shift.wait_send()
    spread_sent(0)
    spread_sent(1)

    @pl.loop(0, BLOCKS)
    def _(b):
        for copy in strip_copies(b):
            copy.wait_send()

    @pl.loop(0, 8)
    def _(j):
        out_copy(j).wait()

    z_out.wait()


def per_device(active_matrix, schur_rows, accum_first, accum_second):
    dma = pltpu.SemaphoreType.DMA
    anywhere = pl.BlockSpec(memory_space=pl.ANY)
    return pl.pallas_call(
        kernel,
        out_shape=(
            jax.ShapeDtypeStruct((ROWS, W), F32),
            jax.ShapeDtypeStruct((ZR, W), F32),
        ),
        in_specs=[anywhere] * 4,
        out_specs=[anywhere] * 2,
        scratch_shapes=[
            pltpu.VMEM((ROWS + ZR, W), F32),
            pltpu.VMEM((2, 16, ROWS), F32),
            pltpu.VMEM((2, W, ROWS), F32),
            pltpu.VMEM((2, W, W), F32),
            pltpu.VMEM((2, W, W), BF16),
            pltpu.VMEM((2, W, W), BF16),
            pltpu.VMEM((ROWS + ZR, 2 * W), F32),
            pltpu.VMEM((W, W), BF16),
            pltpu.VMEM((W, W), BF16),
            pltpu.VMEM((ROWS + W, W), F32),
            pltpu.VMEM((ROWS + ZR, W), F32),
            dma((10,)),
            dma((2, 8)),
            dma((2,)),
            dma((2,)),
            dma((2,)),
            dma((2,)),
            dma((2,)),
            dma((2, 4)),
            dma((2, 4)),
            dma((2, 3)),
            dma((2, 3)),
            dma((2, 4)),
            dma((2, 4)),
            dma((2, 4)),
            dma((2, 4)),
            dma((2, BLOCKS)),
            dma((2, BLOCKS)),
            dma((2,)),
            dma((2,)),
            dma((9,)),
        ],
        compiler_params=pltpu.CompilerParams(
            collective_id=0, has_side_effects=True, vmem_limit_bytes=58 * 1024 * 1024
        ),
        cost_estimate=pl.CostEstimate(flops=14_000_000_000, bytes_accessed=20_000_000, transcendentals=0),
    )(active_matrix, schur_rows, accum_first, accum_second)


def solution(mesh):
    in_specs = (P("row", "col"), P("row", "col"), P("row", "col", None), P("row", "col", None))
    out_specs = (P("row", "col"), P("row", "col"))
    return jax.shard_map(
        per_device, mesh=mesh, in_specs=in_specs, out_specs=out_specs, check_vma=False
    )
```

```python
import jax
import jax.numpy as jnp
from jax import lax
from jax.experimental import pallas as pl
from jax.experimental.pallas import tpu as pltpu
from jax.sharding import PartitionSpec as P

MESH = pl.DeviceIdType.MESH
F32 = jnp.float32
BF16 = jnp.bfloat16

W = 512
HALF = 256
ROWS = 2048
ZR = 256
BLOCKS = (ROWS + ZR) // 256


def split(a):
    high = a.astype(BF16)
    low = (a - high.astype(F32)).astype(BF16)
    return high, low


def product(a, b, dims):
    (a_high, a_low), (b_high, b_low) = a, b

    def dot(left, right):
        return lax.dot_general(left, right, (dims, ((), ())), preferred_element_type=F32)

    return (dot(a_low, b_high) + dot(a_high, b_low)) + dot(a_high, b_high)


def plain(a, b):
    return product(a, b, ((1,), (0,)))


def turned(a, b):
    return product(a, b, ((0,), (0,)))


def remote(src, dst, send, recv, device):
    return pltpu.make_async_remote_copy(
        src_ref=src, dst_ref=dst, send_sem=send, recv_sem=recv, device_id=device, device_id_type=MESH
    )


def at(start, size):
    return pl.ds(pl.multiple_of(start, size), size)


def block_of(position):
    return jnp.where(
        position < 2, position, jnp.where(position < 4, position + 4, jnp.where(position < 8, position - 2, 8))
    )


def window_of(position):
    return jnp.where(position == 0, 0, jnp.where(position == 1, 3, position - 1))


def kernel(
    h_ref, z_ref, u_ref, v_ref, ho_ref, zo_ref,
    tile, piece, gathered, column, col_high, col_low, wide, t_high, t_low, tall, result,
    load_sem, a_send, a_recv, shift_sem, sib_send, sib_recv, own_sem, y_send, y_recv,
    z_send, z_recv, x_send, x_recv, f_send, f_recv, c_send, c_recv, d_send, d_recv, p_sem, detour, out_sem,
):
    r, c = lax.axis_index("row"), lax.axis_index("col")
    hi, y = r // 4, r % 4
    x, z, core = c // 8, (c // 2) % 4, c % 2
    sibling = (r, c + 1 - 2 * core)
    y_next, y_prev = (hi * 4 + (y + 1) % 4, c), (hi * 4 + (y + 3) % 4, c)
    x_next, x_prev = (r, (c + 8) % 32), (r, (c + 24) % 32)
    z_other = [(r, 8 * x + 2 * ((z + d) % 4) + core) for d in (1, 2, 3)]
    c_next, c_prev = (r, (c + 1) % 32), (r, (c + 31) % 32)
    r_next, r_prev = ((r + 1) % 8, c), ((r + 7) % 8, c)
    source_row = c // 4
    to_self = jnp.logical_and(source_row == r, x == y)
    relays = jnp.logical_or(y == 1, y == 2)
    relay_to = (hi * 4 + jnp.where(y == 0, 1, 2), c)
    relay_on = ((1 - hi) * 4 + jnp.where(y == 1, 3, 0), c)
    relay_by = ((1 - hi) * 4 + jnp.where(y == 3, 1, 2), c)
    half = at(core * 1024, 1024)
    other_half = at(1024 - core * 1024, 1024)

    loads = [
        pltpu.make_async_copy(h_ref, tile.at[pl.ds(0, ROWS)], load_sem.at[0]),
        pltpu.make_async_copy(z_ref, tile.at[pl.ds(ROWS, ZR)], load_sem.at[1]),
    ]
    u_loads = [
        pltpu.make_async_copy(u_ref.at[k], piece.at[0, :, pl.ds(W * k, W)], load_sem.at[2 + k]) for k in range(4)
    ]
    v_loads = [
        pltpu.make_async_copy(
            v_ref.at[0, :, pl.ds(HALF, HALF)], piece.at[1, :, pl.ds(0, HALF)], load_sem.at[6]
        )
    ] + [
        pltpu.make_async_copy(v_ref.at[k], piece.at[1, :, pl.ds(W * k - HALF, W)], load_sem.at[6 + k])
        for k in range(1, 4)
    ]
    for copy in u_loads + v_loads + loads:
        copy.start()

    barrier = pltpu.get_barrier_semaphore()
    def hello(device):
        pl.semaphore_signal(barrier, inc=1, device_id=device, device_id_type=MESH)

    for device in [sibling, y_next, y_prev, x_next, x_prev, c_next, c_prev, r_next, r_prev] + z_other:
        hello(device)

    @pl.when(jnp.logical_not(relays))
    def _():
        hello(relay_by)

    for i in range(8):
        source = 8 * y + i

        @pl.when(jnp.logical_not(jnp.logical_and(source_row == r, source == c)))
        def _():
            hello((source_row, source))

    number = jnp.int32
    pl.semaphore_wait(
        barrier,
        20 + relays.astype(number) - to_self.astype(number),
    )

    waits = []

    shift = remote(
        v_ref.at[0, :, pl.ds(0, HALF)], piece.at[1, :, pl.ds(ROWS - HALF, HALF)],
        shift_sem.at[0], shift_sem.at[1], r_prev,
    )
    shift.start()

    def spread_start(t):
        for k in range(4):
            for other in range(2):
                src = piece.at[t, :, pl.ds(W * k, W)]
                dst = column.at[t, at(16 * c, 16), :]
                here = jnp.logical_and(jnp.logical_and(other == hi, x == y), 4 * r + k == c)

                @pl.when(here)
                def _():
                    pltpu.make_async_copy(src, dst, a_recv.at[t]).start()

                @pl.when(jnp.logical_not(here))
                def _():
                    remote(
                        src, dst, a_send.at[t, 2 * k + other], a_recv.at[t], (4 * other + x, 4 * r + k)
                    ).start()

    def spread_sent(t):
        for k in range(4):
            for other in range(2):
                src = piece.at[t, :, pl.ds(W * k, W)]
                dst = column.at[t, at(16 * c, 16), :]
                here = jnp.logical_and(jnp.logical_and(other == hi, x == y), 4 * r + k == c)

                @pl.when(jnp.logical_not(here))
                def _():
                    remote(
                        src, dst, a_send.at[t, 2 * k + other], a_recv.at[t], (4 * other + x, 4 * r + k)
                    ).wait_send()

    def spread_arrived(t):
        group = column.at[t, at(128 * y, 128), :]
        pltpu.make_async_copy(group, group, a_recv.at[t]).wait()

    def ring(t, me, next_device, prev_device, region, part, send, recv):
        def copies(i):
            back, front, far = (i + 3) % 4, (i + 1) % 4, (i + 2) % 4
            out = [
                remote(region(i), region(i), send.at[t, 0], recv.at[t, 0], next_device),
                remote(region(i), region(i), send.at[t, 1], recv.at[t, 1], prev_device),
                remote(part(back, 0), part(back, 0), send.at[t, 2], recv.at[t, 2], next_device),
                remote(part(front, 1), part(front, 1), send.at[t, 3], recv.at[t, 3], prev_device),
            ]
            arrivals = [
                remote(region(back), region(back), send.at[t, 0], recv.at[t, 0], next_device),
                remote(region(front), region(front), send.at[t, 1], recv.at[t, 1], prev_device),
                remote(part(far, 0), part(far, 0), send.at[t, 2], recv.at[t, 2], next_device),
                remote(part(far, 1), part(far, 1), send.at[t, 3], recv.at[t, 3], prev_device),
            ]
            return out, arrivals

        return copies(me)

    y_rings = [
        ring(
            t, y, y_next, y_prev,
            lambda j, t=t: column.at[t, at(128 * j, 128), :],
            lambda j, s, t=t: column.at[t, at(128 * j + 64 * s, 64), :],
            y_send, y_recv,
        )
        for t in range(2)
    ]
    x_rings = [
        ring(
            t, x, x_next, x_prev,
            lambda j, t=t: gathered.at[t, at(128 * j, 128), half],
            lambda j, s, t=t: gathered.at[t, at(128 * j + 64 * s, 64), half],
            x_send, x_recv,
        )
        for t in range(2)
    ]

    def start(copy):
        copy.start()
        waits.append(copy)

    def sibling_start(t):
        start(
            remote(
                piece.at[t, :, other_half], gathered.at[t, at(16 * c, 16), other_half],
                sib_send.at[t], sib_recv.at[t], sibling,
            )
        )
        pltpu.make_async_copy(piece.at[t, :, half], gathered.at[t, at(16 * c, 16), half], own_sem.at[t]).start()

    def sibling_arrived(t):
        rows = at(16 * (c + 1 - 2 * core), 16)
        remote(
            piece.at[t, :, half], gathered.at[t, rows, half], sib_send.at[t], sib_recv.at[t], sibling
        ).wait_recv()
        pltpu.make_async_copy(piece.at[t, :, half], gathered.at[t, at(16 * c, 16), half], own_sem.at[t]).wait()

    def z_start(t):
        ours = gathered.at[t, at(32 * (c // 2), 32), half]
        for i in range(3):
            start(remote(ours, ours, z_send.at[t, i], z_recv.at[t, i], z_other[i]))

    def z_arrived(t):
        for i in range(3):
            theirs = gathered.at[t, at(32 * (4 * x + (z + 3 - i) % 4), 32), half]
            remote(theirs, theirs, z_send.at[t, i], z_recv.at[t, i], z_other[i]).wait_recv()

    def forward(t, j):
        group = gathered.at[t, at(128 * ((x + j) % 4), 128), half]
        start(remote(group, group, f_send.at[t, j], f_recv.at[t, j], sibling))

    def forwarded(t):
        for j in range(4):
            group = gathered.at[t, at(128 * ((x + j) % 4), 128), other_half]
            remote(group, group, f_send.at[t, j], f_recv.at[t, j], sibling).wait_recv()

    def ring_first(ring):
        out, _ = ring
        start(out[0])
        start(out[1])

    def ring_second(ring):
        out, arrivals = ring
        arrivals[0].wait_recv()
        start(out[2])
        arrivals[1].wait_recv()
        start(out[3])

    def ring_last(ring):
        _, arrivals = ring
        arrivals[2].wait_recv()
        arrivals[3].wait_recv()

    def split_column(t):
        high, low = split(column[t])
        col_high[t] = high
        col_low[t] = low

    def strip_copies(b):
        rows = at(256 * b, 256)
        return (
            remote(
                wide.at[rows, pl.ds(256, 256)], wide.at[rows, pl.ds(768, 256)],
                c_send.at[0, b], c_recv.at[0, b], c_prev,
            ),
            remote(
                wide.at[rows, pl.ds(512, 256)], wide.at[rows, pl.ds(0, 256)],
                c_send.at[1, b], c_recv.at[1, b], c_next,
            ),
        )

    def right_first(low, high):
        @pl.loop(low, high)
        def _(position):
            b = block_of(position)
            rows = at(256 * b, 256)
            wide[rows, pl.ds(256, 512)] = plain(split(tile[rows, :]), (col_high[0], col_low[0]))
            for copy in strip_copies(b):
                copy.start()

    def right_second(b, store):
        rows = at(256 * b, 256)
        for copy in strip_copies(b):
            copy.wait_recv()
        for s in range(2):
            cols = pl.ds(256 * s, 256)
            store(
                cols,
                plain(split(wide[rows, pl.ds(512 * s, 512)]), (col_high[1, :, cols], col_low[1, :, cols])),
            )

    def row_strip(way, part):
        src = tall.at[pl.ds((256, 2048)[way] + 128 * part, 128)]
        dst = tall.at[pl.ds((2304, 0)[way] + 128 * part, 128)]
        return remote(src, dst, d_send.at[way, part], d_recv.at[way, part], (r_prev, r_next)[way])

    def row_detour(way):
        src = tall.at[pl.ds((256, 2048)[way] + 128, 128)]
        return remote(src, detour, d_send.at[way, 1], p_sem.at[0], relay_to)

    def row_start(way):
        crosses = y == (0, 3)[way]
        start(row_strip(way, 0))

        @pl.when(crosses)
        def _():
            row_detour(way).start()

        @pl.when(jnp.logical_not(crosses))
        def _():
            row_strip(way, 1).start()

    def row_sent(way):
        row_strip(way, 1).wait_send()

    def row_arrived(way):
        for part in range(2):
            row_strip(way, part).wait_recv()

    def relay(way):
        dst = tall.at[pl.ds((2304, 0)[way] + 128, 128)]
        return remote(detour, dst, p_sem.at[1], d_recv.at[way, 1], relay_on)

    def relay_start():
        for way in range(2):

            @pl.when(y == (1, 2)[way])
            def _():
                remote(detour, detour, p_sem.at[1], p_sem.at[0], relay_to).wait_recv()
                relay(way).start()

    def relay_sent():
        for way in range(2):

            @pl.when(y == (1, 2)[way])
            def _():
                relay(way).wait_send()

    def window(position):
        k = window_of(position)

        @pl.loop(0, 2)
        def _(s):
            def store(cols, value):
                high, low = split(value)
                t_high[at(256 * s, 256), cols] = high
                t_low[at(256 * s, 256), cols] = low

            right_second(2 * k + s, store)

        @pl.loop(0, 2)
        def _(s):
            start_row = 512 * k + 256 * s
            tall[at(256 + start_row, 256), :] = turned(
                split(gathered[0, :, at(start_row, 256)]), (t_high[...], t_low[...])
            )

        if position < 2:
            row_start(position)

    def out_copy(j):
        return pltpu.make_async_copy(
            result.at[at(256 * j, 256)], ho_ref.at[at(256 * j, 256)], out_sem.at[j]
        )

    def left_second(low, high):
        @pl.loop(low, high)
        def _(j):
            result[at(256 * j, 256), :] = turned(
                split(gathered[1, :, at(256 * j, 256)]), split(tall[at(512 * ((j + 1) // 2), 512), :])
            )
            out_copy(j).start()

    for copy in u_loads:
        copy.wait()
    spread_start(0)
    sibling_start(0)
    sibling_arrived(0)
    z_start(0)
    for copy in v_loads:
        copy.wait()
    shift.wait_recv()
    sibling_start(1)
    spread_arrived(0)
    ring_first(y_rings[0])
    sibling_arrived(1)
    z_start(1)
    ring_second(y_rings[0])
    for copy in loads:
        copy.wait()
    ring_last(y_rings[0])
    split_column(0)
    spread_start(1)
    right_first(0, 4)
    z_arrived(0)
    ring_first(x_rings[0])
    forward(0, 0)
    right_first(4, 9)
    spread_arrived(1)
    ring_first(y_rings[1])
    ring_second(x_rings[0])
    forward(0, 3)
    forward(0, 1)
    z_arrived(1)
    ring_first(x_rings[1])
    forward(1, 0)
    ring_second(y_rings[1])
    ring_last(x_rings[0])
    forward(0, 2)
    ring_last(y_rings[1])
    split_column(1)
    forwarded(0)
    window(0)
    ring_second(x_rings[1])
    forward(1, 3)
    forward(1, 1)
    window(1)
    ring_last(x_rings[1])
    forward(1, 2)
    window(2)
    relay_start()
    forwarded(1)
    left_second(1, 3)
    window(3)
    left_second(3, 7)

    def store_z(cols, value):
        result[pl.ds(ROWS, ZR), cols] = value

    right_second(8, store_z)
    z_out = pltpu.make_async_copy(result.at[pl.ds(ROWS, ZR)], zo_ref, out_sem.at[8])
    z_out.start()
    row_arrived(1)
    left_second(0, 1)
    row_arrived(0)
    left_second(7, 8)

    for copy in waits:
        copy.wait_send()
    shift.wait_send()
    for t in range(2):
        spread_sent(t)
        row_sent(t)
    relay_sent()

    @pl.loop(0, BLOCKS)
    def _(b):
        for copy in strip_copies(b):
            copy.wait_send()

    @pl.loop(0, 8)
    def _(j):
        out_copy(j).wait()

    z_out.wait()


def per_device(active_matrix, schur_rows, accum_first, accum_second):
    dma = pltpu.SemaphoreType.DMA
    anywhere = pl.BlockSpec(memory_space=pl.ANY)
    return pl.pallas_call(
        kernel,
        out_shape=(
            jax.ShapeDtypeStruct((ROWS, W), F32),
            jax.ShapeDtypeStruct((ZR, W), F32),
        ),
        in_specs=[anywhere] * 4,
        out_specs=[anywhere] * 2,
        scratch_shapes=[
            pltpu.VMEM((ROWS + ZR, W), F32),
            pltpu.VMEM((2, 16, ROWS), F32),
            pltpu.VMEM((2, W, ROWS), F32),
            pltpu.VMEM((2, W, W), F32),
            pltpu.VMEM((2, W, W), BF16),
            pltpu.VMEM((2, W, W), BF16),
            pltpu.VMEM((ROWS + ZR, 2 * W), F32),
            pltpu.VMEM((W, W), BF16),
            pltpu.VMEM((W, W), BF16),
            pltpu.VMEM((ROWS + W, W), F32),
            pltpu.VMEM((ROWS + ZR, W), F32),
            dma((10,)),
            dma((2, 8)),
            dma((2,)),
            dma((2,)),
            dma((2,)),
            dma((2,)),
            dma((2,)),
            dma((2, 4)),
            dma((2, 4)),
            dma((2, 3)),
            dma((2, 4)),
            dma((2, 4)),
            dma((2, 4)),
            dma((2, 4)),
            dma((2, 4)),
            dma((2, BLOCKS)),
            dma((2, BLOCKS)),
            dma((2, 2)),
            dma((2, 2)),
            dma((2,)),
            pltpu.VMEM((128, W), F32),
            dma((9,)),
        ],
        compiler_params=pltpu.CompilerParams(
            collective_id=0, has_side_effects=True, vmem_limit_bytes=58 * 1024 * 1024
        ),
        cost_estimate=pl.CostEstimate(flops=14_000_000_000, bytes_accessed=20_000_000, transcendentals=0),
    )(active_matrix, schur_rows, accum_first, accum_second)


def solution(mesh):
    in_specs = (P("row", "col"), P("row", "col"), P("row", "col", None), P("row", "col", None))
    out_specs = (P("row", "col"), P("row", "col"))
    return jax.shard_map(
        per_device, mesh=mesh, in_specs=in_specs, out_specs=out_specs, check_vma=False
    )
```

```python
import jax
import jax.numpy as jnp
from jax import lax
from jax.experimental import pallas as pl
from jax.experimental.pallas import tpu as pltpu
from jax.sharding import PartitionSpec as P

MESH = pl.DeviceIdType.MESH
F32 = jnp.float32
BF16 = jnp.bfloat16

W = 512
HALF = 256
ROWS = 2048
ZR = 256
BLOCKS = (ROWS + ZR) // 256


def split(a):
    high = a.astype(BF16)
    low = (a - high.astype(F32)).astype(BF16)
    return high, low


def product(a, b, dims):
    (a_high, a_low), (b_high, b_low) = a, b

    def dot(left, right):
        return lax.dot_general(left, right, (dims, ((), ())), preferred_element_type=F32)

    return (dot(a_low, b_high) + dot(a_high, b_low)) + dot(a_high, b_high)


def plain(a, b):
    return product(a, b, ((1,), (0,)))


def turned(a, b):
    return product(a, b, ((0,), (0,)))


def remote(src, dst, send, recv, device):
    return pltpu.make_async_remote_copy(
        src_ref=src, dst_ref=dst, send_sem=send, recv_sem=recv, device_id=device, device_id_type=MESH
    )


def at(start, size):
    return pl.ds(pl.multiple_of(start, size), size)


def block_of(position):
    return jnp.where(
        position < 2, position, jnp.where(position < 4, position + 4, jnp.where(position < 8, position - 2, 8))
    )


def window_of(position):
    return jnp.where(position == 0, 0, jnp.where(position == 1, 3, position - 1))


def kernel(
    h_ref, z_ref, u_ref, v_ref, ho_ref, zo_ref,
    tile, piece, gathered, column, col_high, col_low, wide, t_high, t_low, tall, result,
    load_sem, a_send, a_recv, shift_sem, sib_send, sib_recv, own_sem, y_send, y_recv,
    z_send, z_recv, x_send, x_recv, f_send, f_recv, c_send, c_recv, d_send, d_recv, p_sem, detour, out_sem,
):
    r, c = lax.axis_index("row"), lax.axis_index("col")
    hi, y = r // 4, r % 4
    x, z, core = c // 8, (c // 2) % 4, c % 2
    sibling = (r, c + 1 - 2 * core)
    y_next, y_prev = (hi * 4 + (y + 1) % 4, c), (hi * 4 + (y + 3) % 4, c)
    x_next, x_prev = (r, (c + 8) % 32), (r, (c + 24) % 32)
    z_other = [(r, 8 * x + 2 * ((z + d) % 4) + core) for d in (1, 2, 3)]
    c_next, c_prev = (r, (c + 1) % 32), (r, (c + 31) % 32)
    r_next, r_prev = ((r + 1) % 8, c), ((r + 7) % 8, c)
    source_row = c // 4
    to_self = jnp.logical_and(source_row == r, x == y)
    relays = jnp.logical_or(y == 1, y == 2)
    relay_to = (hi * 4 + jnp.where(y == 0, 1, 2), c)
    relay_on = ((1 - hi) * 4 + jnp.where(y == 1, 3, 0), c)
    relay_by = ((1 - hi) * 4 + jnp.where(y == 3, 1, 2), c)
    half = at(core * 1024, 1024)
    other_half = at(1024 - core * 1024, 1024)

    loads = [
        pltpu.make_async_copy(h_ref, tile.at[pl.ds(0, ROWS)], load_sem.at[0]),
        pltpu.make_async_copy(z_ref, tile.at[pl.ds(ROWS, ZR)], load_sem.at[1]),
    ]
    u_loads = [
        pltpu.make_async_copy(u_ref.at[k], piece.at[0, :, pl.ds(W * k, W)], load_sem.at[2 + k]) for k in range(4)
    ]
    v_loads = [
        pltpu.make_async_copy(
            v_ref.at[0, :, pl.ds(HALF, HALF)], piece.at[1, :, pl.ds(0, HALF)], load_sem.at[6]
        )
    ] + [
        pltpu.make_async_copy(v_ref.at[k], piece.at[1, :, pl.ds(W * k - HALF, W)], load_sem.at[6 + k])
        for k in range(1, 4)
    ]
    for copy in u_loads + v_loads + loads:
        copy.start()

    barrier = pltpu.get_barrier_semaphore()
    def hello(device):
        pl.semaphore_signal(barrier, inc=1, device_id=device, device_id_type=MESH)

    for device in [sibling, y_next, y_prev, x_next, x_prev, c_next, c_prev, r_next, r_prev] + z_other:
        hello(device)

    @pl.when(jnp.logical_not(relays))
    def _():
        hello(relay_by)

    for i in range(8):
        source = 8 * y + i

        @pl.when(jnp.logical_not(jnp.logical_and(source_row == r, source == c)))
        def _():
            hello((source_row, source))

    number = jnp.int32
    pl.semaphore_wait(
        barrier,
        20 + relays.astype(number) - to_self.astype(number),
    )

    waits = []

    shift = remote(
        v_ref.at[0, :, pl.ds(0, HALF)], piece.at[1, :, pl.ds(ROWS - HALF, HALF)],
        shift_sem.at[0], shift_sem.at[1], r_prev,
    )
    shift.start()

    def spread_start(t):
        for k in range(4):
            for other in range(2):
                src = piece.at[t, :, pl.ds(W * k, W)]
                dst = column.at[t, at(16 * c, 16), :]
                here = jnp.logical_and(jnp.logical_and(other == hi, x == y), 4 * r + k == c)

                @pl.when(here)
                def _():
                    pltpu.make_async_copy(src, dst, a_recv.at[t]).start()

                @pl.when(jnp.logical_not(here))
                def _():
                    remote(
                        src, dst, a_send.at[t, 2 * k + other], a_recv.at[t], (4 * other + x, 4 * r + k)
                    ).start()

    def spread_sent(t):
        for k in range(4):
            for other in range(2):
                src = piece.at[t, :, pl.ds(W * k, W)]
                dst = column.at[t, at(16 * c, 16), :]
                here = jnp.logical_and(jnp.logical_and(other == hi, x == y), 4 * r + k == c)

                @pl.when(jnp.logical_not(here))
                def _():
                    remote(
                        src, dst, a_send.at[t, 2 * k + other], a_recv.at[t], (4 * other + x, 4 * r + k)
                    ).wait_send()

    def spread_arrived(t):
        group = column.at[t, at(128 * y, 128), :]
        pltpu.make_async_copy(group, group, a_recv.at[t]).wait()

    def ring(t, me, next_device, prev_device, region, part, send, recv, all_prev, all_next):
        def copies(i):
            back, front, far = (i + 3) % 4, (i + 1) % 4, (i + 2) % 4
            def pick(condition, yes, no):
                return tuple(jnp.where(condition, a, b) for a, b in zip(yes, no))

            first = part(jnp.where(all_prev, front, back), 0)
            second = part(jnp.where(all_next, back, front), 1)
            out = [
                remote(region(i), region(i), send.at[t, 0], recv.at[t, 0], next_device),
                remote(region(i), region(i), send.at[t, 1], recv.at[t, 1], prev_device),
                remote(first, first, send.at[t, 2], recv.at[t, 2], pick(all_prev, prev_device, next_device)),
                remote(second, second, send.at[t, 3], recv.at[t, 3], pick(all_next, next_device, prev_device)),
            ]
            arrivals = [
                remote(region(back), region(back), send.at[t, 0], recv.at[t, 0], next_device),
                remote(region(front), region(front), send.at[t, 1], recv.at[t, 1], prev_device),
                remote(part(far, 0), part(far, 0), send.at[t, 2], recv.at[t, 2], next_device),
                remote(part(far, 1), part(far, 1), send.at[t, 3], recv.at[t, 3], prev_device),
            ]
            return out, arrivals

        return copies(me)

    y_rings = [
        ring(
            t, y, y_next, y_prev,
            lambda j, t=t: column.at[t, at(128 * j, 128), :],
            lambda j, s, t=t: column.at[t, at(128 * j + 64 * s, 64), :],
            y_send, y_recv, False, False,
        )
        for t in range(2)
    ]
    x_rings = [
        ring(
            t, x, x_next, x_prev,
            lambda j, t=t: gathered.at[t, at(128 * j, 128), half],
            lambda j, s, t=t: gathered.at[t, at(128 * j + 64 * s, 64), half],
            x_send, x_recv, jnp.logical_and(t == 1, z == 0), jnp.logical_and(t == 1, z == 3),
        )
        for t in range(2)
    ]

    def start(copy):
        copy.start()
        waits.append(copy)

    def sibling_start(t):
        start(
            remote(
                piece.at[t, :, other_half], gathered.at[t, at(16 * c, 16), other_half],
                sib_send.at[t], sib_recv.at[t], sibling,
            )
        )
        pltpu.make_async_copy(piece.at[t, :, half], gathered.at[t, at(16 * c, 16), half], own_sem.at[t]).start()

    def sibling_arrived(t):
        rows = at(16 * (c + 1 - 2 * core), 16)
        remote(
            piece.at[t, :, half], gathered.at[t, rows, half], sib_send.at[t], sib_recv.at[t], sibling
        ).wait_recv()
        pltpu.make_async_copy(piece.at[t, :, half], gathered.at[t, at(16 * c, 16), half], own_sem.at[t]).wait()

    def z_start(t):
        ours = gathered.at[t, at(32 * (c // 2), 32), half]
        for i in range(3):
            start(remote(ours, ours, z_send.at[t, i], z_recv.at[t, i], z_other[i]))

    def z_arrived(t):
        for i in range(3):
            theirs = gathered.at[t, at(32 * (4 * x + (z + 3 - i) % 4), 32), half]
            remote(theirs, theirs, z_send.at[t, i], z_recv.at[t, i], z_other[i]).wait_recv()

    def forward(t, j):
        group = gathered.at[t, at(128 * ((x + j) % 4), 128), half]
        start(remote(group, group, f_send.at[t, j], f_recv.at[t, j], sibling))

    def forwarded(t):
        for j in range(4):
            group = gathered.at[t, at(128 * ((x + j) % 4), 128), other_half]
            remote(group, group, f_send.at[t, j], f_recv.at[t, j], sibling).wait_recv()

    def ring_first(ring):
        out, _ = ring
        start(out[0])
        start(out[1])

    def ring_second(ring, one_way=False):
        out, arrivals = ring
        arrivals[0].wait_recv()
        if one_way:
            arrivals[1].wait_recv()
        start(out[2])
        if not one_way:
            arrivals[1].wait_recv()
        start(out[3])

    def ring_last(ring):
        _, arrivals = ring
        arrivals[2].wait_recv()
        arrivals[3].wait_recv()

    def split_column(t):
        high, low = split(column[t])
        col_high[t] = high
        col_low[t] = low

    def strip_copies(b):
        rows = at(256 * b, 256)
        return (
            remote(
                wide.at[rows, pl.ds(256, 256)], wide.at[rows, pl.ds(768, 256)],
                c_send.at[0, b], c_recv.at[0, b], c_prev,
            ),
            remote(
                wide.at[rows, pl.ds(512, 256)], wide.at[rows, pl.ds(0, 256)],
                c_send.at[1, b], c_recv.at[1, b], c_next,
            ),
        )

    def right_first(low, high):
        @pl.loop(low, high)
        def _(position):
            b = block_of(position)
            rows = at(256 * b, 256)
            wide[rows, pl.ds(256, 512)] = plain(split(tile[rows, :]), (col_high[0], col_low[0]))
            for copy in strip_copies(b):
                copy.start()

    def right_second(b, store):
        rows = at(256 * b, 256)
        for copy in strip_copies(b):
            copy.wait_recv()
        for s in range(2):
            cols = pl.ds(256 * s, 256)
            store(
                cols,
                plain(split(wide[rows, pl.ds(512 * s, 512)]), (col_high[1, :, cols], col_low[1, :, cols])),
            )

    def row_strip(way, part):
        src = tall.at[pl.ds((256, 2048)[way] + 128 * part, 128)]
        dst = tall.at[pl.ds((2304, 0)[way] + 128 * part, 128)]
        return remote(src, dst, d_send.at[way, part], d_recv.at[way, part], (r_prev, r_next)[way])

    def row_detour(way):
        src = tall.at[pl.ds((256, 2048)[way] + 128, 128)]
        return remote(src, detour, d_send.at[way, 1], p_sem.at[0], relay_to)

    def row_start(way):
        crosses = y == (0, 3)[way]
        start(row_strip(way, 0))

        @pl.when(crosses)
        def _():
            row_detour(way).start()

        @pl.when(jnp.logical_not(crosses))
        def _():
            row_strip(way, 1).start()

    def row_sent(way):
        row_strip(way, 1).wait_send()

    def row_arrived(way):
        for part in range(2):
            row_strip(way, part).wait_recv()

    def relay(way):
        dst = tall.at[pl.ds((2304, 0)[way] + 128, 128)]
        return remote(detour, dst, p_sem.at[1], d_recv.at[way, 1], relay_on)

    def relay_start():
        for way in range(2):

            @pl.when(y == (1, 2)[way])
            def _():
                remote(detour, detour, p_sem.at[1], p_sem.at[0], relay_to).wait_recv()
                relay(way).start()

    def relay_sent():
        for way in range(2):

            @pl.when(y == (1, 2)[way])
            def _():
                relay(way).wait_send()

    def window(position):
        k = window_of(position)

        @pl.loop(0, 2)
        def _(s):
            def store(cols, value):
                high, low = split(value)
                t_high[at(256 * s, 256), cols] = high
                t_low[at(256 * s, 256), cols] = low

            right_second(2 * k + s, store)

        @pl.loop(0, 2)
        def _(s):
            start_row = 512 * k + 256 * s
            tall[at(256 + start_row, 256), :] = turned(
                split(gathered[0, :, at(start_row, 256)]), (t_high[...], t_low[...])
            )

        if position < 2:
            row_start(position)

    def out_copy(j):
        return pltpu.make_async_copy(
            result.at[at(256 * j, 256)], ho_ref.at[at(256 * j, 256)], out_sem.at[j]
        )

    def left_second(low, high):
        @pl.loop(low, high)
        def _(j):
            result[at(256 * j, 256), :] = turned(
                split(gathered[1, :, at(256 * j, 256)]), split(tall[at(512 * ((j + 1) // 2), 512), :])
            )
            out_copy(j).start()

    for copy in u_loads:
        copy.wait()
    spread_start(0)
    sibling_start(0)
    sibling_arrived(0)
    z_start(0)
    for copy in v_loads:
        copy.wait()
    shift.wait_recv()
    sibling_start(1)
    spread_arrived(0)
    ring_first(y_rings[0])
    sibling_arrived(1)
    z_start(1)
    ring_second(y_rings[0])
    for copy in loads:
        copy.wait()
    ring_last(y_rings[0])
    split_column(0)
    spread_start(1)
    right_first(0, 4)
    z_arrived(0)
    ring_first(x_rings[0])
    forward(0, 0)
    right_first(4, 9)
    spread_arrived(1)
    ring_first(y_rings[1])
    ring_second(x_rings[0])
    forward(0, 3)
    forward(0, 1)
    z_arrived(1)
    ring_first(x_rings[1])
    forward(1, 0)
    ring_second(y_rings[1])
    ring_last(x_rings[0])
    forward(0, 2)
    ring_last(y_rings[1])
    split_column(1)
    forwarded(0)
    window(0)
    ring_second(x_rings[1], one_way=True)
    forward(1, 3)
    forward(1, 1)
    window(1)
    ring_last(x_rings[1])
    forward(1, 2)
    window(2)
    relay_start()
    forwarded(1)
    left_second(1, 3)
    window(3)
    left_second(3, 7)

    def store_z(cols, value):
        result[pl.ds(ROWS, ZR), cols] = value

    right_second(8, store_z)
    z_out = pltpu.make_async_copy(result.at[pl.ds(ROWS, ZR)], zo_ref, out_sem.at[8])
    z_out.start()
    row_arrived(1)
    left_second(0, 1)
    row_arrived(0)
    left_second(7, 8)

    for copy in waits:
        copy.wait_send()
    shift.wait_send()
    for t in range(2):
        spread_sent(t)
        row_sent(t)
    relay_sent()

    @pl.loop(0, BLOCKS)
    def _(b):
        for copy in strip_copies(b):
            copy.wait_send()

    @pl.loop(0, 8)
    def _(j):
        out_copy(j).wait()

    z_out.wait()


def per_device(active_matrix, schur_rows, accum_first, accum_second):
    dma = pltpu.SemaphoreType.DMA
    anywhere = pl.BlockSpec(memory_space=pl.ANY)
    return pl.pallas_call(
        kernel,
        out_shape=(
            jax.ShapeDtypeStruct((ROWS, W), F32),
            jax.ShapeDtypeStruct((ZR, W), F32),
        ),
        in_specs=[anywhere] * 4,
        out_specs=[anywhere] * 2,
        scratch_shapes=[
            pltpu.VMEM((ROWS + ZR, W), F32),
            pltpu.VMEM((2, 16, ROWS), F32),
            pltpu.VMEM((2, W, ROWS), F32),
            pltpu.VMEM((2, W, W), F32),
            pltpu.VMEM((2, W, W), BF16),
            pltpu.VMEM((2, W, W), BF16),
            pltpu.VMEM((ROWS + ZR, 2 * W), F32),
            pltpu.VMEM((W, W), BF16),
            pltpu.VMEM((W, W), BF16),
            pltpu.VMEM((ROWS + W, W), F32),
            pltpu.VMEM((ROWS + ZR, W), F32),
            dma((10,)),
            dma((2, 8)),
            dma((2,)),
            dma((2,)),
            dma((2,)),
            dma((2,)),
            dma((2,)),
            dma((2, 4)),
            dma((2, 4)),
            dma((2, 3)),
            dma((2, 4)),
            dma((2, 4)),
            dma((2, 4)),
            dma((2, 4)),
            dma((2, 4)),
            dma((2, BLOCKS)),
            dma((2, BLOCKS)),
            dma((2, 2)),
            dma((2, 2)),
            dma((2,)),
            pltpu.VMEM((128, W), F32),
            dma((9,)),
        ],
        compiler_params=pltpu.CompilerParams(
            collective_id=0, has_side_effects=True, vmem_limit_bytes=58 * 1024 * 1024
        ),
        cost_estimate=pl.CostEstimate(flops=14_000_000_000, bytes_accessed=20_000_000, transcendentals=0),
    )(active_matrix, schur_rows, accum_first, accum_second)


def solution(mesh):
    in_specs = (P("row", "col"), P("row", "col"), P("row", "col", None), P("row", "col", None))
    out_specs = (P("row", "col"), P("row", "col"))
    return jax.shard_map(
        per_device, mesh=mesh, in_specs=in_specs, out_specs=out_specs, check_vma=False
    )
```
